32 devices in a mesh: enc: 2 (over core), row: 4 (over y, x), col: 4 (over z).
Axes of the slice: x: 2, y: 2, z: 4, core: 2. Of those that a mesh axis runs over, the one named last changes fastest.
Arguments:
- embedding: bfloat16 [16, 256, 256], P(('row', 'col'), 'enc'), may hold values from -6 to 6
- w_first: bfloat16 [256, 256], replicated, may hold values from -0.375 to 0.375
- b_first: float32 [256], replicated, may hold values from -3 to 3
- w_second: bfloat16 [256, 256], replicated, may hold values from -0.375 to 0.375
- w_layer: bfloat16 [256, 256], replicated, may hold values from -0.375 to 0.375
- block_source: int32 [16, 48], P(('row', 'col')), may hold values from 0 to 15, as said below
- block_rows: int32 [16, 48], P(('row', 'col')), may hold values from 0 to 1
- block_cols: int32 [16, 48], P(('row', 'col')), may hold values from 0 to 1
- block_count: int32 [16], P(('row', 'col')), may hold values from 3 to 48, as said below
- block_tiles: bfloat16 [16, 48, 128, 128], P(('row', 'col')), may hold values from -0.15625 to 0.15625
- node_order: int32 [4, 4, 256], P(None, 'col'), may hold values from 0 to 255, each once within a row
- cotangent: bfloat16 [16, 256, 256], P(('row', 'col'), None, 'enc'), may hold values from -9 to 9
Outputs:
- activated: bfloat16 [16, 256, 256], P(('row', 'col'), None, 'enc')
- grad_layer: float32 [256, 256], replicated
- grad_embed: float32 [16, 256, 256], P(('row', 'col'), 'enc')
The draws below stay inside these ranges and needn't reach their ends.
Inputs may be any that keep to these rules, and one draw needn't show every extreme that they name: `block_source`: the slots of target s come in 16 runs of 3 slots; the slots of one run name the same source segment, different runs name different ones, and the first run names s itself. `block_count`: at least one target segment has all 48 slots live.
All inputs are finite; a program needn't handle non-finite values.
Results may differ from the reference program's by a relative error of at most 0.01.
Values may be sent and summed in bfloat16 or wider, within the bound.
A program may use at most 128 MiB of HBM per device.

```python
import jax
import jax.numpy as jnp
from jax import lax

EMBED_WIDTH = 256
TILE_SIZE = 128
SEG_ROWS = 256
SEGMENTS = 16
ALL_NODES = 4096
ROW_BLOCKS = 2
PAIR_SLOTS = 3
LIST_GROUPS = 16
LIST_SLOTS = 48
N_ROW = 4
N_COL = 4


def draw_block_source(key, part):
    key = jax.random.fold_in(key, 5)
    row_keys = jax.random.split(key, SEGMENTS)
    shuffled = jax.vmap(lambda one_key: jax.random.permutation(one_key, SEGMENTS - 1))(row_keys)
    offsets = jnp.concatenate([jnp.zeros((SEGMENTS, 1), jnp.int32), shuffled[:, :LIST_GROUPS - 1].astype(jnp.int32) + 1], axis=1)
    sources = (jnp.arange(SEGMENTS, dtype=jnp.int32)[:, None] + offsets) % SEGMENTS
    return jnp.repeat(sources, PAIR_SLOTS, axis=1).astype(jnp.int32)


def draw_block_count(key, part):
    key = jax.random.fold_in(key, 11)
    key_drawn, key_full = jax.random.split(key, 2)
    counted = jax.random.randint(key_drawn, (SEGMENTS,), PAIR_SLOTS, LIST_SLOTS + 1)
    full_at = jax.random.randint(key_full, (), 0, SEGMENTS)
    counted = counted.at[full_at].set(LIST_SLOTS)
    return counted.astype(jnp.int32)


def draw_cotangent(key, part):
    key = jax.random.fold_in(key, 23)
    key_main = jax.random.fold_in(key, 0)
    growth = 3.0 ** (jnp.arange(SEGMENTS, dtype=jnp.float32) / max(SEGMENTS - 1, 1))
    normal_part = jax.random.normal(key_main, (SEGMENTS, SEG_ROWS, EMBED_WIDTH), jnp.float32)
    normal_part = jnp.clip(normal_part, -3.0, 3.0)
    return (normal_part * growth[:, None, None]).astype(jnp.bfloat16)


def set_ends(values, rng, least, largest):
    longest = values.shape.index(max(values.shape))
    spots = []
    for shift in (0, 1):
        where = [jax.random.randint(jax.random.fold_in(rng, axis), (), 0, length) for axis, length in enumerate(values.shape)]
        where[longest] = (where[longest] + shift) % values.shape[longest]
        spots.append(tuple(where))
    return values.at[spots[0]].set(least).at[spots[1]].set(largest)


def steps_of(own_key, extent, shards, smallest, largest):
    def one(axis_at, blocks):
        steps = jax.random.uniform(jax.random.fold_in(jax.random.fold_in(own_key, 6), axis_at), (blocks,), jnp.float32, smallest / len(shards), largest / len(shards))
        return jnp.repeat(jnp.exp(steps), extent[axis_at] // blocks).reshape((-1,) + (1,) * (len(extent) - axis_at - 1))

    loudness = one(*shards[0])
    for cut in shards[1:]:
        loudness = loudness * one(*cut)
    return loudness


def centred(own_key, dims, width, limit, cuts=(), kind=jnp.bfloat16):
    result = width * jax.random.normal(own_key, dims, jnp.float32)
    if cuts:
        result = result * steps_of(own_key, dims, cuts, -0.22, 0.18)
    return jnp.clip(result, -limit, limit).astype(kind)


def setup_inputs(seed: int = 0) -> dict:
    key_list = jax.random.split(jax.random.key(seed), 13)
    embedding = centred(key_list[0], (SEGMENTS, SEG_ROWS, EMBED_WIDTH), 1.0, 6.0, ((0, 16), (1, 2)))
    w_first = centred(key_list[1], (EMBED_WIDTH, EMBED_WIDTH), EMBED_WIDTH ** -0.5, 0.375)
    b_first = centred(key_list[2], (EMBED_WIDTH,), 0.5, 3.0, (), jnp.float32)
    w_second = centred(key_list[3], (EMBED_WIDTH, EMBED_WIDTH), EMBED_WIDTH ** -0.5, 0.375)
    w_layer = centred(key_list[4], (EMBED_WIDTH, EMBED_WIDTH), EMBED_WIDTH ** -0.5, 0.375)
    block_source = draw_block_source(jax.random.fold_in(key_list[12], 71), 0)
    block_rows = set_ends(jax.random.randint(key_list[6], (SEGMENTS, LIST_SLOTS), 0, ROW_BLOCKS), jax.random.fold_in(key_list[6], 1), 0, ROW_BLOCKS - 1).astype(jnp.int32)
    block_cols = set_ends(jax.random.randint(key_list[7], (SEGMENTS, LIST_SLOTS), 0, ROW_BLOCKS), jax.random.fold_in(key_list[7], 1), 0, ROW_BLOCKS - 1).astype(jnp.int32)
    block_count = draw_block_count(jax.random.fold_in(key_list[12], 71), 0)
    block_tiles = centred(key_list[9], (SEGMENTS, LIST_SLOTS, TILE_SIZE, TILE_SIZE), (LIST_SLOTS * TILE_SIZE * TILE_SIZE // (2 * SEG_ROWS)) ** -0.5, 0.15625, ((0, 16),))
    node_order = jax.vmap(lambda own: jax.random.permutation(own, SEG_ROWS))(jax.random.split(key_list[10], N_ROW * N_COL)).reshape((N_ROW, N_COL, SEG_ROWS)).astype(jnp.int32)
    cotangent = draw_cotangent(jax.random.fold_in(key_list[12], 71), 0)
    return dict(embedding=embedding, w_first=w_first, b_first=b_first, w_second=w_second, w_layer=w_layer, block_source=block_source, block_rows=block_rows, block_cols=block_cols, block_count=block_count, block_tiles=block_tiles, node_order=node_order, cotangent=cotangent)


def silu_slope(values):
    sigmoid = jax.nn.sigmoid(values)
    return sigmoid * (1.0 + values * (1.0 - sigmoid))


def reference(embedding, w_first, b_first, w_second, w_layer, block_source, block_rows, block_cols, block_count, block_tiles, node_order, cotangent):
    node_table = embedding.reshape(ALL_NODES, EMBED_WIDTH)
    first_linear = jnp.dot(node_table, w_first, preferred_element_type=jnp.float32) + b_first
    hidden_first = jax.nn.silu(first_linear).astype(jnp.bfloat16)
    encoded = jnp.dot(hidden_first, w_second, preferred_element_type=jnp.float32).astype(jnp.bfloat16)
    projected = jnp.dot(encoded, w_layer, preferred_element_type=jnp.float32).astype(jnp.bfloat16)
    node_perm = node_order.reshape(SEGMENTS, SEG_ROWS)
    grid_rows = jnp.take_along_axis(projected.reshape(SEGMENTS, SEG_ROWS, EMBED_WIDTH), node_perm[:, :, None], axis=1)
    grid_blocks = grid_rows.reshape(SEGMENTS * ROW_BLOCKS, TILE_SIZE, EMBED_WIDTH)
    slot_index = jnp.arange(LIST_SLOTS, dtype=jnp.int32)

    def forward_one(packed):
        slot_src, slot_rows, slot_cols, slot_count, slot_tiles = packed
        flat_index = (slot_src * ROW_BLOCKS + slot_cols).astype(jnp.int32)
        source_blocks = jnp.take(grid_blocks, flat_index, axis=0).astype(jnp.float32)
        products = jnp.einsum("lij,ljf->lif", slot_tiles.astype(jnp.float32), source_blocks)
        live_mask = (slot_index < slot_count).astype(jnp.float32)
        row_pick = jax.nn.one_hot(slot_rows, ROW_BLOCKS, dtype=jnp.float32) * live_mask[:, None]
        summed = jnp.einsum("lr,lif->rif", row_pick, products, precision=lax.Precision.HIGHEST)
        return summed.reshape(SEG_ROWS, EMBED_WIDTH)

    aggregated = lax.map(forward_one, (block_source, block_rows, block_cols, block_count, block_tiles))
    activated = jax.nn.silu(aggregated).astype(jnp.bfloat16)
    pre_grad = (cotangent.astype(jnp.float32) * silu_slope(aggregated)).astype(jnp.bfloat16)
    grad_blocks = pre_grad.reshape(SEGMENTS, ROW_BLOCKS, TILE_SIZE, EMBED_WIDTH)

    def backward_one(running_sum, packed):
        slot_src, slot_rows, slot_cols, slot_count, slot_tiles, own_blocks = packed
        gathered = jnp.take(own_blocks, slot_rows, axis=0).astype(jnp.float32)
        products = jnp.einsum("lji,ljf->lif", slot_tiles.astype(jnp.float32), gathered)
        live_mask = (slot_index < slot_count).astype(jnp.float32)
        products = products * live_mask[:, None, None]
        put_index = (slot_src * ROW_BLOCKS + slot_cols).astype(jnp.int32)
        return running_sum.at[put_index].add(products), None

    start_sum = jnp.zeros((SEGMENTS * ROW_BLOCKS, TILE_SIZE, EMBED_WIDTH), jnp.float32)
    grid_sum, _ = lax.scan(backward_one, start_sum, (block_source, block_rows, block_cols, block_count, block_tiles, grad_blocks))
    grid_grad = grid_sum.reshape(SEGMENTS, SEG_ROWS, EMBED_WIDTH)
    seg_index = jnp.arange(SEGMENTS, dtype=jnp.int32)[:, None]
    positions = jnp.broadcast_to(jnp.arange(SEG_ROWS, dtype=jnp.int32)[None, :], (SEGMENTS, SEG_ROWS))
    inverse = jnp.zeros((SEGMENTS, SEG_ROWS), jnp.int32).at[seg_index, node_perm].set(positions)
    node_grad = jnp.take_along_axis(grid_grad, inverse[:, :, None], axis=1)
    projected_grad = node_grad.reshape(ALL_NODES, EMBED_WIDTH).astype(jnp.bfloat16)
    grad_layer = jnp.dot(encoded.T, projected_grad, preferred_element_type=jnp.float32)
    encoded_grad = jnp.dot(projected_grad, w_layer.T, preferred_element_type=jnp.float32).astype(jnp.bfloat16)
    hidden_grad = (jnp.dot(encoded_grad, w_second.T, preferred_element_type=jnp.float32) * silu_slope(first_linear)).astype(jnp.bfloat16)
    grad_embed = jnp.dot(hidden_grad, w_first.T, preferred_element_type=jnp.float32).reshape(SEGMENTS, SEG_ROWS, EMBED_WIDTH)
    return activated, grad_layer, grad_embed
```

```python
import functools

import jax
import jax.numpy as jnp
from jax import lax
from jax.experimental import pallas as pl
from jax.experimental.pallas import tpu as pltpu
from jax.sharding import PartitionSpec as P

MESH = pl.DeviceIdType.MESH
PAIR = 3
F32 = jnp.float32
BF16 = jnp.bfloat16


def silu_slope(values):
    sigmoid = jax.nn.sigmoid(values)
    return sigmoid * (1.0 + values * (1.0 - sigmoid))


def dot(a, b, ca=1, cb=0):
    return lax.dot_general(a, b, (((ca,), (cb,)), ((), ())), preferred_element_type=F32)


def kernel(n_row, n_col, emb, w1, b1, w2, wl, meta, tiles, order, cot,
           act_o, gl_o, ge_o,
           first, pall, psend, eall, pgx, pgsend, feat, acc, pgt, pb, rb, sb, cb, own,
           glp, glr, glc, glf,
           m_send, m_recv, fc_send, fr_send, f_recv, br_send, br_recv, bc_send, bc_recv,
           g1_send, g1_recv, g2_send, g2_recv, g3_send, g3_recv):
    me_e = lax.axis_index("enc")
    me_r = lax.axis_index("row")
    me_c = lax.axis_index("col")
    mate = 1 - me_e
    half = emb.shape[0]
    rows = 2 * half
    width = pall.shape[2]
    ts = tiles.shape[1]

    def row_of(d):
        return lax.rem(me_r + d, n_row)

    def col_of(d):
        return lax.rem(me_c + d, n_col)

    def remote(src, dst, ssem, rsem, **dev):
        return pltpu.make_async_remote_copy(
            src_ref=src, dst_ref=dst, send_sem=ssem, recv_sem=rsem,
            device_id=dev, device_id_type=MESH)

    barrier = pltpu.get_barrier_semaphore()
    pl.semaphore_signal(barrier, inc=1, device_id={"enc": mate}, device_id_type=MESH)
    for d in range(1, n_row):
        for e in range(2):
            pl.semaphore_signal(barrier, inc=1, device_id={"enc": e, "row": row_of(d)},
                                device_id_type=MESH)
    for d in range(1, n_col):
        pl.semaphore_signal(barrier, inc=1, device_id={"col": col_of(d)}, device_id_type=MESH)

    linear = dot(emb[...], w1[...]) + b1[...]
    first[...] = linear
    hidden = (linear * jax.nn.sigmoid(linear)).astype(BF16)
    encoded = dot(hidden, w2[...]).astype(BF16)
    eall[me_e] = encoded
    projected = dot(encoded, wl[...]).astype(BF16)
    psend[0] = projected[:, :width]
    psend[1] = projected[:, width:]
    pall[me_e] = psend[me_e]
    node_ids = lax.broadcasted_iota(jnp.int32, (rows, rows), 0)
    perm_t = jnp.where(node_ids == order[me_r], 1.0, 0.0).astype(BF16)

    pl.semaphore_wait(barrier, 2 * n_row - 1 + n_col - 1)
    copy_p = remote(psend.at[mate], pall.at[me_e], m_send.at[0], m_recv.at[0], enc=mate)
    copy_p.start()
    copy_e = remote(eall.at[me_e], eall.at[me_e], m_send.at[1], m_recv.at[1], enc=mate)
    copy_e.start()
    copy_p.wait()

    me_slot = me_r * n_col + me_c
    grid_own = dot(perm_t, pall[...].reshape(rows, width), 0, 0).astype(BF16)
    feat[me_slot] = grid_own.reshape(rows // ts, ts, width)

    def feat_col(d):
        slot = me_r * n_col + me_c
        return remote(feat.at[slot], feat.at[slot], fc_send.at[d], f_recv.at[slot], col=col_of(d))

    def feat_row(dc, dr):
        slot = me_r * n_col + col_of(dc)
        return remote(feat.at[slot], feat.at[slot], fr_send.at[dc * n_row + dr],
                      f_recv.at[slot], row=row_of(dr))

    def feat_wait(slot):
        remote(feat.at[slot], feat.at[slot], fc_send.at[0], f_recv.at[slot], enc=mate).wait_recv()

    for d in range(1, n_col):
        feat_col(d).start()
    for d in range(1, n_row):
        feat_row(0, d).start()

    def slots(seg):
        out = []
        for k in range(PAIR):
            m = meta[seg * PAIR + k]
            live = (m & 1) == 1
            out.append((m >> 3, live, (m >> 1) & 1, (m >> 2) & 1))
        return out

    def split(tile, live, which, axis):
        zero = jnp.zeros_like(tile)
        return jnp.concatenate(
            [jnp.where(jnp.logical_and(live, which == b), tile, zero) for b in range(rows // ts)],
            axis=axis)

    def pick(blocks, c):
        chosen = blocks[0]
        for b in range(1, len(blocks)):
            chosen = jnp.where(c == b, blocks[b], chosen)
        return chosen

    def forward(seg):
        lhs, rhs = [], []
        for index, live, r, c in slots(seg):
            lhs.append(split(tiles[index], live, r, 0))
            rhs.append(pick([feat[seg, b] for b in range(rows // ts)], c))
        return dot(jnp.concatenate(lhs, axis=1), jnp.concatenate(rhs, axis=0))

    acc[...] = forward(me_slot)

    def relay(dc, carry):
        slot = me_r * n_col + col_of(dc)
        feat_wait(slot)
        for d in range(1, n_row):
            feat_row(dc, d).start()
        acc[...] += forward(slot)
        return carry

    lax.fori_loop(1, n_col, relay, 0)

    def take(step, carry):
        dc = step // (n_row - 1)
        dr = step % (n_row - 1) + 1
        slot = row_of(dr) * n_col + col_of(dc)
        feat_wait(slot)
        acc[...] += forward(slot)
        return carry

    lax.fori_loop(0, n_col * (n_row - 1), take, 0)

    aggregated = acc[...]
    sig = jax.nn.sigmoid(aggregated)
    act_o[...] = (aggregated * sig).astype(BF16)
    slope = sig * (1.0 + aggregated * (1.0 - sig))
    pre = cot[...].astype(F32) * slope
    for b in range(rows // ts):
        pgt[b] = pre[b * ts:(b + 1) * ts].T.astype(BF16)

    def backward(seg):
        lhs, rhs = [], []
        for index, live, r, c in slots(seg):
            lhs.append(pgt[r])
            rhs.append(split(tiles[index], live, c, 1))
        return dot(jnp.concatenate(lhs, axis=1), jnp.concatenate(rhs, axis=0))

    def back_row(dc, dr):
        slot = row_of(dr) * n_col + col_of(dc)
        there = me_r * n_col + col_of(dc)
        return remote(pb.at[slot], rb.at[there], br_send.at[dc * n_row + dr],
                      br_recv.at[there], row=row_of(dr))

    def give(step, carry):
        dc = lax.rem(step // (n_row - 1) + 1, n_col)
        dr = step % (n_row - 1) + 1
        slot = row_of(dr) * n_col + col_of(dc)
        pb[slot] = backward(slot).astype(BF16)
        back_row(dc, dr).start()
        return carry

    lax.fori_loop(0, n_col * (n_row - 1), give, 0)

    def row_total(dc):
        total = backward(me_r * n_col + col_of(dc))
        for dr in range(1, n_row):
            slot = row_of(dr) * n_col + col_of(dc)
            remote(rb.at[slot], rb.at[slot], br_send.at[0], br_recv.at[slot], enc=mate).wait_recv()
            total = total + rb[slot].astype(F32)
        return total

    def back_col(dc):
        return remote(sb.at[dc], cb.at[me_c], bc_send.at[dc], bc_recv.at[me_c], col=col_of(dc))

    def pass_on(dc, carry):
        sb[dc] = row_total(dc).astype(BF16)
        back_col(dc).start()
        return carry

    lax.fori_loop(1, n_col, pass_on, 0)
    own[...] = row_total(0)

    def collect(dc, carry):
        at = col_of(dc)
        remote(cb.at[at], cb.at[at], bc_send.at[0], bc_recv.at[at], enc=mate).wait_recv()
        own[...] += cb[at].astype(F32)
        return carry

    lax.fori_loop(1, n_col, collect, 0)

    grid_grad = own[...].astype(BF16)
    node_grad = dot(perm_t, grid_grad, 1, 1).astype(BF16)
    pgsend[...] = node_grad.reshape(2, half, width)
    copy_g = remote(pgsend.at[mate], pgx.at[me_e], m_send.at[2], m_recv.at[2], enc=mate)
    copy_g.start()
    pgx[me_e] = pgsend[me_e]

    copy_e.wait()
    part = dot(eall[...].reshape(rows, eall.shape[2]), node_grad, 0, 0)
    chunk = glp.shape[1]
    glp[...] = part.astype(BF16).reshape(n_row, chunk, width)

    def gl_row(d):
        to = row_of(d)
        return remote(glp.at[to], glr.at[me_r], g1_send.at[d], g1_recv.at[me_r], row=to)

    for d in range(1, n_row):
        gl_row(d).start()

    copy_g.wait()
    full_grad = jnp.concatenate([pgx[0], pgx[1]], axis=1)
    encoded_grad = dot(full_grad, wl[...], 1, 1).astype(BF16)
    hidden_grad = (dot(encoded_grad, w2[...], 1, 1) * silu_slope(first[...])).astype(BF16)
    ge_o[...] = dot(hidden_grad, w1[...], 1, 1)

    total = glp[me_r].astype(F32)
    for d in range(1, n_row):
        at = row_of(d)
        remote(glr.at[at], glr.at[at], g1_send.at[0], g1_recv.at[at], enc=mate).wait_recv()
        total = total + glr[at].astype(F32)
    glc[me_c] = total.astype(BF16)

    def gl_col(d):
        return remote(glc.at[me_c], glc.at[me_c], g2_send.at[d], g2_recv.at[me_c], col=col_of(d))

    for d in range(1, n_col):
        gl_col(d).start()
    for d in range(1, n_col):
        at = col_of(d)
        remote(glc.at[at], glc.at[at], g2_send.at[0], g2_recv.at[at], enc=mate).wait_recv()
    total = glc[0].astype(F32)
    for c in range(1, n_col):
        total = total + glc[c].astype(F32)
    mine = me_e * n_row + me_r
    glf[mine] = total.astype(BF16)

    def gl_all(de, dr):
        return remote(glf.at[mine], glf.at[mine], g3_send.at[de * n_row + dr], g3_recv.at[mine],
                      enc=lax.rem(me_e + de, 2), row=row_of(dr))

    others = [(de, dr) for de in range(2) for dr in range(n_row) if de or dr]
    for de, dr in others:
        gl_all(de, dr).start()
    for de, dr in others:
        at = lax.rem(me_e + de, 2) * n_row + row_of(dr)
        remote(glf.at[at], glf.at[at], g3_send.at[0], g3_recv.at[at], enc=mate).wait_recv()
    for e in range(2):
        for r in range(n_row):
            gl_o[r * chunk:(r + 1) * chunk, e * width:(e + 1) * width] = (
                glf[e * n_row + r].astype(F32))

    for d in range(1, n_col):
        feat_col(d).wait_send()
        back_col(d).wait_send()
        gl_col(d).wait_send()
    for d in range(1, n_row):
        gl_row(d).wait_send()
    for de, dr in others:
        gl_all(de, dr).wait_send()

    def drain(step, carry):
        dc = step // (n_row - 1)
        dr = step % (n_row - 1) + 1
        feat_row(dc, dr).wait_send()
        back_row(dc, dr).wait_send()
        return carry

    lax.fori_loop(0, n_col * (n_row - 1), drain, 0)


def on_device(embedding, w_first, b_first, w_second, w_layer, block_source, block_rows,
              block_cols, block_count, block_tiles, node_order, cotangent):
    n_row = lax.axis_size("row")
    n_col = lax.axis_size("col")
    segs = n_row * n_col
    half = embedding.shape[1]
    full = embedding.shape[2]
    rows = 2 * half
    width = full // 2
    ts = block_tiles.shape[-1]
    blocks = rows // ts
    total = block_source.shape[1]

    slot = jnp.arange(total, dtype=jnp.int32)
    live = (slot < block_count[0]).astype(jnp.int32)
    value = (live + block_rows[0] * 2 + block_cols[0] * 4 + slot * 8).reshape(-1, PAIR)
    sources = block_source[0].reshape(-1, PAIR)
    match = sources[None, :, :] == jnp.arange(segs, dtype=jnp.int32)[:, None, None]
    meta = jnp.sum(jnp.where(match, value[None], 0), axis=1).reshape(segs * PAIR)

    vmem = pl.BlockSpec(memory_space=pltpu.VMEM)
    smem = pl.BlockSpec(memory_space=pltpu.SMEM)
    dma = pltpu.SemaphoreType.DMA
    chunk = full // n_row
    scratch = [
        pltpu.VMEM((half, full), F32),
        pltpu.VMEM((2, half, width), BF16),
        pltpu.VMEM((2, half, width), BF16),
        pltpu.VMEM((2, half, full), BF16),
        pltpu.VMEM((2, half, width), BF16),
        pltpu.VMEM((2, half, width), BF16),
        pltpu.VMEM((segs, blocks, ts, width), BF16),
        pltpu.VMEM((rows, width), F32),
        pltpu.VMEM((blocks, width, ts), BF16),
        pltpu.VMEM((segs, width, rows), BF16),
        pltpu.VMEM((segs, width, rows), BF16),
        pltpu.VMEM((n_col, width, rows), BF16),
        pltpu.VMEM((n_col, width, rows), BF16),
        pltpu.VMEM((width, rows), F32),
        pltpu.VMEM((n_row, chunk, width), BF16),
        pltpu.VMEM((n_row, chunk, width), BF16),
        pltpu.VMEM((n_col, chunk, width), BF16),
        pltpu.VMEM((2 * n_row, chunk, width), BF16),
        dma((3,)), dma((3,)),
        dma((n_col,)), dma((segs,)), dma((segs,)),
        dma((segs,)), dma((segs,)), dma((n_col,)), dma((n_col,)),
        dma((n_row,)), dma((n_row,)), dma((n_col,)), dma((n_col,)),
        dma((2 * n_row,)), dma((2 * n_row,)),
    ]
    activated, grad_layer, grad_embed = pl.pallas_call(
        functools.partial(kernel, n_row, n_col),
        out_shape=(
            jax.ShapeDtypeStruct((rows, width), BF16),
            jax.ShapeDtypeStruct((full, full), F32),
            jax.ShapeDtypeStruct((half, full), F32),
        ),
        in_specs=[vmem, vmem, vmem, vmem, vmem, smem, vmem, vmem, vmem],
        out_specs=(vmem, vmem, vmem),
        scratch_shapes=scratch,
        compiler_params=pltpu.CompilerParams(
            collective_id=0, has_side_effects=True, vmem_limit_bytes=48 * 1024 * 1024),
    )(embedding[0], w_first, b_first[None], w_second, w_layer, meta, block_tiles[0],
      node_order, cotangent[0])
    return (activated[None], grad_layer, grad_embed[None])


def solution(mesh):
    in_specs = (
        P(("row", "col"), "enc", None),
        P(),
        P(),
        P(),
        P(),
        P(("row", "col"), None),
        P(("row", "col"), None),
        P(("row", "col"), None),
        P(("row", "col")),
        P(("row", "col"), None, None, None),
        P(None, "col", None),
        P(("row", "col"), None, "enc"),
    )
    out_specs = (P(("row", "col"), None, "enc"), P(), P(("row", "col"), "enc", None))
    return jax.shard_map(
        on_device, mesh=mesh, in_specs=in_specs, out_specs=out_specs, check_vma=False
    )
```

```python
import functools

import jax
import jax.numpy as jnp
from jax import lax
from jax.experimental import pallas as pl
from jax.experimental.pallas import tpu as pltpu
from jax.sharding import PartitionSpec as P

MESH = pl.DeviceIdType.MESH
PAIR = 3
F32 = jnp.float32
BF16 = jnp.bfloat16


def silu_slope(values):
    sigmoid = jax.nn.sigmoid(values)
    return sigmoid * (1.0 + values * (1.0 - sigmoid))


def dot(a, b, ca=1, cb=0):
    return lax.dot_general(a, b, (((ca,), (cb,)), ((), ())), preferred_element_type=F32)


def kernel(n_row, n_col, emb_h, w1_h, b1_h, w2_h, wl_h, src, rws, cls, cnt, tiles_h, order_h, cot_h,
           act_o, gl_o, ge_o,
           emb, w1, b1, w2, wl, tiles, order, cot, meta, in_sem,
           first, pall, psend, eall, pgx, pgsend, feat, acc, pgt, pb, rb, sb, cb, own,
           glp, glr, glc, glf,
           m_send, m_recv, fc_send, fr_send, f_recv, br_send, br_recv, bc_send, bc_recv,
           g1_send, g1_recv, g2_send, g2_recv, g3_send, g3_recv):
    me_e = lax.axis_index("enc")
    me_r = lax.axis_index("row")
    me_c = lax.axis_index("col")
    mate = 1 - me_e
    half = emb.shape[0]
    rows = 2 * half
    width = pall.shape[2]
    ts = tiles.shape[1]

    def row_of(d):
        return lax.rem(me_r + d, n_row)

    def col_of(d):
        return lax.rem(me_c + d, n_col)

    def remote(src, dst, ssem, rsem, **dev):
        return pltpu.make_async_remote_copy(
            src_ref=src, dst_ref=dst, send_sem=ssem, recv_sem=rsem,
            device_id=dev, device_id_type=MESH)

    pairs = [(emb_h, emb), (w1_h, w1), (b1_h, b1), (w2_h, w2), (wl_h, wl), (order_h, order),
             (tiles_h, tiles), (cot_h, cot)]
    loads = [pltpu.make_async_copy(a, b, in_sem.at[i]) for i, (a, b) in enumerate(pairs)]
    for load in loads:
        load.start()

    barrier = pltpu.get_barrier_semaphore()
    pl.semaphore_signal(barrier, inc=1, device_id={"enc": mate}, device_id_type=MESH)
    for d in range(1, n_row):
        for e in range(2):
            pl.semaphore_signal(barrier, inc=1, device_id={"enc": e, "row": row_of(d)},
                                device_id_type=MESH)
    for d in range(1, n_col):
        pl.semaphore_signal(barrier, inc=1, device_id={"col": col_of(d)}, device_id_type=MESH)

    runs = src.shape[1] // PAIR

    def tabulate(seg, carry):
        at = jnp.int32(0)
        there = jnp.int32(0)
        for j in range(runs):
            hit = src[0, j * PAIR] == seg
            at = jnp.where(hit, j * PAIR, at)
            there = jnp.where(hit, 1, there)
        for k in range(PAIR):
            slot = at + k
            live = jnp.where(slot < cnt[0], there, 0)
            meta[seg * PAIR + k] = live + rws[0, slot] * 2 + cls[0, slot] * 4 + slot * 8
        return carry

    lax.fori_loop(0, n_row * n_col, tabulate, 0)

    for load in loads[:6]:
        load.wait()
    linear = dot(emb[...], w1[...]) + b1[...]
    first[...] = linear
    hidden = (linear * jax.nn.sigmoid(linear)).astype(BF16)
    encoded = dot(hidden, w2[...]).astype(BF16)
    eall[me_e] = encoded
    projected = dot(encoded, wl[...]).astype(BF16)
    psend[0] = projected[:, :width]
    psend[1] = projected[:, width:]
    pall[me_e] = psend[me_e]
    node_ids = lax.broadcasted_iota(jnp.int32, (rows, rows), 0)
    perm_t = jnp.where(node_ids == order[me_r], 1.0, 0.0).astype(BF16)

    pl.semaphore_wait(barrier, 2 * n_row - 1 + n_col - 1)
    copy_p = remote(psend.at[mate], pall.at[me_e], m_send.at[0], m_recv.at[0], enc=mate)
    copy_p.start()
    copy_e = remote(eall.at[me_e], eall.at[me_e], m_send.at[1], m_recv.at[1], enc=mate)
    copy_e.start()
    copy_p.wait()

    me_slot = me_r * n_col + me_c
    grid_own = dot(perm_t, pall[...].reshape(rows, width), 0, 0).astype(BF16)
    feat[me_slot] = grid_own.reshape(rows // ts, ts, width)

    def feat_col(d):
        slot = me_r * n_col + me_c
        return remote(feat.at[slot], feat.at[slot], fc_send.at[d], f_recv.at[slot], col=col_of(d))

    def feat_row(dc, dr):
        slot = me_r * n_col + col_of(dc)
        return remote(feat.at[slot], feat.at[slot], fr_send.at[dc * n_row + dr],
                      f_recv.at[slot], row=row_of(dr))

    def feat_wait(slot):
        remote(feat.at[slot], feat.at[slot], fc_send.at[0], f_recv.at[slot], enc=mate).wait_recv()

    for d in range(1, n_col):
        feat_col(d).start()
    for d in range(1, n_row):
        feat_row(0, d).start()

    def slots(seg):
        out = []
        for k in range(PAIR):
            m = meta[seg * PAIR + k]
            live = (m & 1) == 1
            out.append((m >> 3, live, (m >> 1) & 1, (m >> 2) & 1))
        return out

    def split(tile, live, which, axis):
        zero = jnp.zeros_like(tile)
        return jnp.concatenate(
            [jnp.where(jnp.logical_and(live, which == b), tile, zero) for b in range(rows // ts)],
            axis=axis)

    def pick(blocks, c):
        chosen = blocks[0]
        for b in range(1, len(blocks)):
            chosen = jnp.where(c == b, blocks[b], chosen)
        return chosen

    def forward(seg):
        lhs, rhs = [], []
        for index, live, r, c in slots(seg):
            lhs.append(split(tiles[index], live, r, 0))
            rhs.append(pick([feat[seg, b] for b in range(rows // ts)], c))
        return dot(jnp.concatenate(lhs, axis=1), jnp.concatenate(rhs, axis=0))

    loads[6].wait()
    acc[...] = forward(me_slot)

    def relay(dc, carry):
        slot = me_r * n_col + col_of(dc)
        feat_wait(slot)
        for d in range(1, n_row):
            feat_row(dc, d).start()
        acc[...] += forward(slot)
        return carry

    lax.fori_loop(1, n_col, relay, 0)

    def take(step, carry):
        dc = step // (n_row - 1)
        dr = step % (n_row - 1) + 1
        slot = row_of(dr) * n_col + col_of(dc)
        feat_wait(slot)
        acc[...] += forward(slot)
        return carry

    lax.fori_loop(0, n_col * (n_row - 1), take, 0)

    loads[7].wait()
    aggregated = acc[...]
    sig = jax.nn.sigmoid(aggregated)
    act_o[...] = (aggregated * sig).astype(BF16)
    slope = sig * (1.0 + aggregated * (1.0 - sig))
    pre = cot[...].astype(F32) * slope
    for b in range(rows // ts):
        pgt[b] = pre[b * ts:(b + 1) * ts].T.astype(BF16)

    def backward(seg):
        lhs, rhs = [], []
        for index, live, r, c in slots(seg):
            lhs.append(pgt[r])
            rhs.append(split(tiles[index], live, c, 1))
        return dot(jnp.concatenate(lhs, axis=1), jnp.concatenate(rhs, axis=0))

    def back_row(dc, dr):
        slot = row_of(dr) * n_col + col_of(dc)
        there = me_r * n_col + col_of(dc)
        return remote(pb.at[slot], rb.at[there], br_send.at[dc * n_row + dr],
                      br_recv.at[there], row=row_of(dr))

    def give(step, carry):
        dc = lax.rem(step // (n_row - 1) + 1, n_col)
        dr = step % (n_row - 1) + 1
        slot = row_of(dr) * n_col + col_of(dc)
        pb[slot] = backward(slot).astype(BF16)
        back_row(dc, dr).start()
        return carry

    lax.fori_loop(0, n_col * (n_row - 1), give, 0)

    def row_total(dc):
        total = backward(me_r * n_col + col_of(dc))
        for dr in range(1, n_row):
            slot = row_of(dr) * n_col + col_of(dc)
            remote(rb.at[slot], rb.at[slot], br_send.at[0], br_recv.at[slot], enc=mate).wait_recv()
            total = total + rb[slot].astype(F32)
        return total

    def back_col(dc):
        return remote(sb.at[dc], cb.at[me_c], bc_send.at[dc], bc_recv.at[me_c], col=col_of(dc))

    def pass_on(dc, carry):
        sb[dc] = row_total(dc).astype(BF16)
        back_col(dc).start()
        return carry

    lax.fori_loop(1, n_col, pass_on, 0)
    own[...] = row_total(0)

    def collect(dc, carry):
        at = col_of(dc)
        remote(cb.at[at], cb.at[at], bc_send.at[0], bc_recv.at[at], enc=mate).wait_recv()
        own[...] += cb[at].astype(F32)
        return carry

    lax.fori_loop(1, n_col, collect, 0)

    grid_grad = own[...].astype(BF16)
    node_grad = dot(perm_t, grid_grad, 1, 1).astype(BF16)
    pgsend[...] = node_grad.reshape(2, half, width)
    copy_g = remote(pgsend.at[mate], pgx.at[me_e], m_send.at[2], m_recv.at[2], enc=mate)
    copy_g.start()
    pgx[me_e] = pgsend[me_e]

    copy_e.wait()
    part = dot(eall[...].reshape(rows, eall.shape[2]), node_grad, 0, 0)
    chunk = glp.shape[1]
    glp[...] = part.astype(BF16).reshape(n_row, chunk, width)

    def gl_row(d):
        to = row_of(d)
        return remote(glp.at[to], glr.at[me_r], g1_send.at[d], g1_recv.at[me_r], row=to)

    for d in range(1, n_row):
        gl_row(d).start()

    copy_g.wait()
    full_grad = jnp.concatenate([pgx[0], pgx[1]], axis=1)
    encoded_grad = dot(full_grad, wl[...], 1, 1).astype(BF16)
    hidden_grad = (dot(encoded_grad, w2[...], 1, 1) * silu_slope(first[...])).astype(BF16)
    ge_o[...] = dot(hidden_grad, w1[...], 1, 1)

    total = glp[me_r].astype(F32)
    for d in range(1, n_row):
        at = row_of(d)
        remote(glr.at[at], glr.at[at], g1_send.at[0], g1_recv.at[at], enc=mate).wait_recv()
        total = total + glr[at].astype(F32)
    glc[me_c] = total.astype(BF16)

    def gl_col(d):
        return remote(glc.at[me_c], glc.at[me_c], g2_send.at[d], g2_recv.at[me_c], col=col_of(d))

    for d in range(1, n_col):
        gl_col(d).start()
    for d in range(1, n_col):
        at = col_of(d)
        remote(glc.at[at], glc.at[at], g2_send.at[0], g2_recv.at[at], enc=mate).wait_recv()
    total = glc[0].astype(F32)
    for c in range(1, n_col):
        total = total + glc[c].astype(F32)
    mine = me_e * n_row + me_r
    glf[mine] = total.astype(BF16)

    def gl_all(de, dr):
        return remote(glf.at[mine], glf.at[mine], g3_send.at[de * n_row + dr], g3_recv.at[mine],
                      enc=lax.rem(me_e + de, 2), row=row_of(dr))

    others = [(de, dr) for de in range(2) for dr in range(n_row) if de or dr]
    for de, dr in others:
        gl_all(de, dr).start()
    for de, dr in others:
        at = lax.rem(me_e + de, 2) * n_row + row_of(dr)
        remote(glf.at[at], glf.at[at], g3_send.at[0], g3_recv.at[at], enc=mate).wait_recv()
    for e in range(2):
        for r in range(n_row):
            gl_o[r * chunk:(r + 1) * chunk, e * width:(e + 1) * width] = (
                glf[e * n_row + r].astype(F32))

    for d in range(1, n_col):
        feat_col(d).wait_send()
        back_col(d).wait_send()
        gl_col(d).wait_send()
    for d in range(1, n_row):
        gl_row(d).wait_send()
    for de, dr in others:
        gl_all(de, dr).wait_send()

    def drain(step, carry):
        dc = step // (n_row - 1)
        dr = step % (n_row - 1) + 1
        feat_row(dc, dr).wait_send()
        back_row(dc, dr).wait_send()
        return carry

    lax.fori_loop(0, n_col * (n_row - 1), drain, 0)


def on_device(embedding, w_first, b_first, w_second, w_layer, block_source, block_rows,
              block_cols, block_count, block_tiles, node_order, cotangent):
    n_row = lax.axis_size("row")
    n_col = lax.axis_size("col")
    segs = n_row * n_col
    half = embedding.shape[1]
    full = embedding.shape[2]
    rows = 2 * half
    width = full // 2
    ts = block_tiles.shape[-1]
    blocks = rows // ts
    total = block_tiles.shape[1]
    vmem = pl.BlockSpec(memory_space=pltpu.VMEM)
    hbm = pl.BlockSpec(memory_space=pltpu.HBM)
    smem = pl.BlockSpec(memory_space=pltpu.SMEM)
    dma = pltpu.SemaphoreType.DMA
    chunk = full // n_row
    scratch = [
        pltpu.VMEM((half, full), BF16),
        pltpu.VMEM((full, full), BF16),
        pltpu.VMEM((1, full), F32),
        pltpu.VMEM((full, full), BF16),
        pltpu.VMEM((full, full), BF16),
        pltpu.VMEM((total, ts, ts), BF16),
        pltpu.VMEM(node_order.shape, jnp.int32),
        pltpu.VMEM((rows, width), BF16),
        pltpu.SMEM((segs * PAIR,), jnp.int32),
        dma((8,)),
        pltpu.VMEM((half, full), F32),
        pltpu.VMEM((2, half, width), BF16),
        pltpu.VMEM((2, half, width), BF16),
        pltpu.VMEM((2, half, full), BF16),
        pltpu.VMEM((2, half, width), BF16),
        pltpu.VMEM((2, half, width), BF16),
        pltpu.VMEM((segs, blocks, ts, width), BF16),
        pltpu.VMEM((rows, width), F32),
        pltpu.VMEM((blocks, width, ts), BF16),
        pltpu.VMEM((segs, width, rows), BF16),
        pltpu.VMEM((segs, width, rows), BF16),
        pltpu.VMEM((n_col, width, rows), BF16),
        pltpu.VMEM((n_col, width, rows), BF16),
        pltpu.VMEM((width, rows), F32),
        pltpu.VMEM((n_row, chunk, width), BF16),
        pltpu.VMEM((n_row, chunk, width), BF16),
        pltpu.VMEM((n_col, chunk, width), BF16),
        pltpu.VMEM((2 * n_row, chunk, width), BF16),
        dma((3,)), dma((3,)),
        dma((n_col,)), dma((segs,)), dma((segs,)),
        dma((segs,)), dma((segs,)), dma((n_col,)), dma((n_col,)),
        dma((n_row,)), dma((n_row,)), dma((n_col,)), dma((n_col,)),
        dma((2 * n_row,)), dma((2 * n_row,)),
    ]
    activated, grad_layer, grad_embed = pl.pallas_call(
        functools.partial(kernel, n_row, n_col),
        out_shape=(
            jax.ShapeDtypeStruct((rows, width), BF16),
            jax.ShapeDtypeStruct((full, full), F32),
            jax.ShapeDtypeStruct((half, full), F32),
        ),
        in_specs=[hbm] * 5 + [smem] * 4 + [hbm] * 3,
        out_specs=(vmem, vmem, vmem),
        scratch_shapes=scratch,
        compiler_params=pltpu.CompilerParams(
            collective_id=0, has_side_effects=True, vmem_limit_bytes=64 * 1024 * 1024),
    )(embedding[0], w_first, b_first[None], w_second, w_layer, block_source,
      block_rows, block_cols, block_count, block_tiles[0], node_order, cotangent[0])
    return (activated[None], grad_layer, grad_embed[None])


def solution(mesh):
    in_specs = (
        P(("row", "col"), "enc", None),
        P(),
        P(),
        P(),
        P(),
        P(("row", "col"), None),
        P(("row", "col"), None),
        P(("row", "col"), None),
        P(("row", "col")),
        P(("row", "col"), None, None, None),
        P(None, "col", None),
        P(("row", "col"), None, "enc"),
    )
    out_specs = (P(("row", "col"), None, "enc"), P(), P(("row", "col"), "enc", None))
    return jax.shard_map(
        on_device, mesh=mesh, in_specs=in_specs, out_specs=out_specs, check_vma=False
    )
```

```python
import functools

import jax
import jax.numpy as jnp
from jax import lax
from jax.experimental import pallas as pl
from jax.experimental.pallas import tpu as pltpu
from jax.sharding import PartitionSpec as P

MESH = pl.DeviceIdType.MESH
PAIR = 3
F32 = jnp.float32
BF16 = jnp.bfloat16


def silu_slope(values):
    sigmoid = jax.nn.sigmoid(values)
    return sigmoid * (1.0 + values * (1.0 - sigmoid))


def dot(a, b, ca=1, cb=0):
    return lax.dot_general(a, b, (((ca,), (cb,)), ((), ())), preferred_element_type=F32)


def kernel(n_row, n_col, emb_h, w1_h, b1_h, w2_h, wl_h, src, rws, cls, cnt, tiles_h, order_h, cot_h,
           act_h, gl_h, ge_h,
           act_o, gl_o, ge_o, out_sem,
           emb, w1, b1, w2, wl, tiles, order, cot, meta, in_sem,
           first, pall, psend, eall, pgx, pgsend, feat, acc, pgt, pb, rb, sb, cb, own,
           glp, glr, glc, glf,
           m_send, m_recv, fc_send, fr_send, f_recv, br_send, br_recv, bc_send, bc_recv,
           g1_send, g1_recv, g2_send, g2_recv, g3_send, g3_recv):
    me_e = lax.axis_index("enc")
    me_r = lax.axis_index("row")
    me_c = lax.axis_index("col")
    mate = 1 - me_e
    half = emb.shape[0]
    rows = 2 * half
    width = pall.shape[2]
    ts = tiles.shape[1]

    def row_of(d):
        return lax.rem(me_r + d, n_row)

    def col_of(d):
        return lax.rem(me_c + d, n_col)

    def remote(src, dst, ssem, rsem, **dev):
        return pltpu.make_async_remote_copy(
            src_ref=src, dst_ref=dst, send_sem=ssem, recv_sem=rsem,
            device_id=dev, device_id_type=MESH)

    pairs = [(emb_h, emb), (w1_h, w1), (b1_h, b1), (w2_h, w2), (wl_h, wl), (order_h, order),
             (tiles_h, tiles), (cot_h, cot)]
    loads = [pltpu.make_async_copy(a, b, in_sem.at[i]) for i, (a, b) in enumerate(pairs)]
    for load in loads:
        load.start()

    barrier = pltpu.get_barrier_semaphore()
    pl.semaphore_signal(barrier, inc=1, device_id={"enc": mate}, device_id_type=MESH)
    for d in range(1, n_row):
        for e in range(2):
            pl.semaphore_signal(barrier, inc=1, device_id={"enc": e, "row": row_of(d)},
                                device_id_type=MESH)
    for d in range(1, n_col):
        pl.semaphore_signal(barrier, inc=1, device_id={"col": col_of(d)}, device_id_type=MESH)

    runs = src.shape[1] // PAIR

    def tabulate(seg, carry):
        at = jnp.int32(0)
        there = jnp.int32(0)
        for j in range(runs):
            hit = src[0, j * PAIR] == seg
            at = jnp.where(hit, j * PAIR, at)
            there = jnp.where(hit, 1, there)
        for k in range(PAIR):
            slot = at + k
            live = jnp.where(slot < cnt[0], there, 0)
            meta[seg * PAIR + k] = live + rws[0, slot] * 2 + cls[0, slot] * 4 + slot * 8
        return carry

    lax.fori_loop(0, n_row * n_col, tabulate, 0)

    for load in loads[:6]:
        load.wait()
    linear = dot(emb[...], w1[...]) + b1[...]
    first[...] = linear
    hidden = (linear * jax.nn.sigmoid(linear)).astype(BF16)
    encoded = dot(hidden, w2[...]).astype(BF16)
    eall[me_e] = encoded
    projected = dot(encoded, wl[...]).astype(BF16)
    psend[0] = projected[:, :width]
    psend[1] = projected[:, width:]
    pall[me_e] = psend[me_e]
    node_ids = lax.broadcasted_iota(jnp.int32, (rows, rows), 0)
    perm_t = jnp.where(node_ids == order[me_r], 1.0, 0.0).astype(BF16)

    pl.semaphore_wait(barrier, 2 * n_row - 1 + n_col - 1)
    copy_p = remote(psend.at[mate], pall.at[me_e], m_send.at[0], m_recv.at[0], enc=mate)
    copy_p.start()
    copy_e = remote(eall.at[me_e], eall.at[me_e], m_send.at[1], m_recv.at[1], enc=mate)
    copy_e.start()
    copy_p.wait()

    me_slot = me_r * n_col + me_c
    grid_own = dot(perm_t, pall[...].reshape(rows, width), 0, 0).astype(BF16)
    feat[me_slot] = grid_own.reshape(rows // ts, ts, width)

    def feat_col(c, step):
        slot = me_r * n_col + c
        return remote(feat.at[slot], feat.at[slot], fc_send.at[(step + 1) // 2 * n_col + c],
                      f_recv.at[slot], col=lax.rem(me_c + step + n_col, n_col))

    def feat_row(dc, dr):
        slot = me_r * n_col + dc
        return remote(feat.at[slot], feat.at[slot], fr_send.at[dc * n_row + dr],
                      f_recv.at[slot], row=row_of(dr))

    def feat_wait(slot):
        remote(feat.at[slot], feat.at[slot], fc_send.at[0], f_recv.at[slot], enc=mate).wait_recv()

    @pl.when(me_c < n_col - 1)
    def _():
        feat_col(me_c, 1).start()

    @pl.when(me_c > 0)
    def _():
        feat_col(me_c, -1).start()

    for d in range(1, n_row):
        feat_row(me_c, d).start()

    def slots(seg):
        out = []
        for k in range(PAIR):
            m = meta[seg * PAIR + k]
            live = (m & 1) == 1
            out.append((m >> 3, live, (m >> 1) & 1, (m >> 2) & 1))
        return out

    def split(tile, live, which, axis):
        zero = jnp.zeros_like(tile)
        return jnp.concatenate(
            [jnp.where(jnp.logical_and(live, which == b), tile, zero) for b in range(rows // ts)],
            axis=axis)

    def pick(blocks, c):
        chosen = blocks[0]
        for b in range(1, len(blocks)):
            chosen = jnp.where(c == b, blocks[b], chosen)
        return chosen

    def forward(seg):
        lhs, rhs = [], []
        for index, live, r, c in slots(seg):
            lhs.append(split(tiles[index], live, r, 0))
            rhs.append(pick([feat[seg, b] for b in range(rows // ts)], c))
        return dot(jnp.concatenate(lhs, axis=1), jnp.concatenate(rhs, axis=0))

    loads[6].wait()
    acc[...] = forward(me_slot)

    def relay(d, carry):
        left = me_c - d
        right = me_c + d

        @pl.when(left >= 0)
        def _():
            feat_wait(me_r * n_col + left)

            @pl.when(me_c < n_col - 1)
            def _():
                feat_col(left, 1).start()

            for dr in range(1, n_row):
                feat_row(left, dr).start()

        @pl.when(right < n_col)
        def _():
            feat_wait(me_r * n_col + right)

            @pl.when(me_c > 0)
            def _():
                feat_col(right, -1).start()

            for dr in range(1, n_row):
                feat_row(right, dr).start()

        @pl.when(left >= 0)
        def _():
            acc[...] += forward(me_r * n_col + left)

        @pl.when(right < n_col)
        def _():
            acc[...] += forward(me_r * n_col + right)

        return carry

    lax.fori_loop(1, n_col, relay, 0)

    def nearest(k):
        low = jnp.minimum(me_c, n_col - 1 - me_c)
        d = (k + 1) // 2
        near = jnp.where(k % 2 == 1, me_c - d, me_c + d)
        far = jnp.where(me_c > n_col - 1 - me_c, n_col - 1 - k, k)
        return jnp.where(k <= 2 * low, near, far)

    def take(step, carry):
        dr = step % (n_row - 1) + 1
        slot = row_of(dr) * n_col + nearest(step // (n_row - 1))
        feat_wait(slot)
        acc[...] += forward(slot)
        return carry

    lax.fori_loop(0, n_col * (n_row - 1), take, 0)

    loads[7].wait()
    aggregated = acc[...]
    sig = jax.nn.sigmoid(aggregated)
    act_o[...] = (aggregated * sig).astype(BF16)
    act_copy = pltpu.make_async_copy(act_o, act_h, out_sem.at[0])
    act_copy.start()
    slope = sig * (1.0 + aggregated * (1.0 - sig))
    pre = cot[...].astype(F32) * slope
    for b in range(rows // ts):
        pgt[b] = pre[b * ts:(b + 1) * ts].T.astype(BF16)

    def backward(seg):
        lhs, rhs = [], []
        for index, live, r, c in slots(seg):
            lhs.append(pgt[r])
            rhs.append(split(tiles[index], live, c, 1))
        return dot(jnp.concatenate(lhs, axis=1), jnp.concatenate(rhs, axis=0))

    def back_row(dc, dr):
        slot = row_of(dr) * n_col + col_of(dc)
        there = me_r * n_col + col_of(dc)
        return remote(pb.at[slot], rb.at[there], br_send.at[dc * n_row + dr],
                      br_recv.at[there], row=row_of(dr))

    def give(step, carry):
        dc = lax.rem(step // (n_row - 1) + 1, n_col)
        dr = step % (n_row - 1) + 1
        slot = row_of(dr) * n_col + col_of(dc)
        pb[slot] = backward(slot).astype(BF16)
        back_row(dc, dr).start()
        return carry

    lax.fori_loop(0, n_col * (n_row - 1), give, 0)

    def row_total(dc):
        total = backward(me_r * n_col + col_of(dc))
        for dr in range(1, n_row):
            slot = row_of(dr) * n_col + col_of(dc)
            remote(rb.at[slot], rb.at[slot], br_send.at[0], br_recv.at[slot], enc=mate).wait_recv()
            total = total + rb[slot].astype(F32)
        return total

    def back_col(dc):
        return remote(sb.at[dc], cb.at[me_c], bc_send.at[dc], bc_recv.at[me_c], col=col_of(dc))

    def pass_on(dc, carry):
        sb[dc] = row_total(dc).astype(BF16)
        back_col(dc).start()
        return carry

    lax.fori_loop(1, n_col, pass_on, 0)
    own[...] = row_total(0)

    def collect(dc, carry):
        at = col_of(dc)
        remote(cb.at[at], cb.at[at], bc_send.at[0], bc_recv.at[at], enc=mate).wait_recv()
        own[...] += cb[at].astype(F32)
        return carry

    lax.fori_loop(1, n_col, collect, 0)

    grid_grad = own[...].astype(BF16)
    node_grad = dot(perm_t, grid_grad, 1, 1).astype(BF16)
    pgsend[...] = node_grad.reshape(2, half, width)
    copy_g = remote(pgsend.at[mate], pgx.at[me_e], m_send.at[2], m_recv.at[2], enc=mate)
    copy_g.start()
    pgx[me_e] = pgsend[me_e]

    copy_e.wait()
    part = dot(eall[...].reshape(rows, eall.shape[2]), node_grad, 0, 0)
    chunk = glp.shape[1]
    glp[...] = part.astype(BF16).reshape(n_row, chunk, width)

    def gl_row(d):
        to = row_of(d)
        return remote(glp.at[to], glr.at[me_r], g1_send.at[d], g1_recv.at[me_r], row=to)

    for d in range(1, n_row):
        gl_row(d).start()

    copy_g.wait()
    full_grad = jnp.concatenate([pgx[0], pgx[1]], axis=1)
    encoded_grad = dot(full_grad, wl[...], 1, 1).astype(BF16)
    hidden_grad = (dot(encoded_grad, w2[...], 1, 1) * silu_slope(first[...])).astype(BF16)
    ge_o[...] = dot(hidden_grad, w1[...], 1, 1)
    ge_copy = pltpu.make_async_copy(ge_o, ge_h, out_sem.at[2])
    ge_copy.start()

    total = glp[me_r].astype(F32)
    for d in range(1, n_row):
        at = row_of(d)
        remote(glr.at[at], glr.at[at], g1_send.at[0], g1_recv.at[at], enc=mate).wait_recv()
        total = total + glr[at].astype(F32)
    glc[me_c] = total.astype(BF16)

    def gl_col(d):
        return remote(glc.at[me_c], glc.at[me_c], g2_send.at[d], g2_recv.at[me_c], col=col_of(d))

    for d in range(1, n_col):
        gl_col(d).start()
    for d in range(1, n_col):
        at = col_of(d)
        remote(glc.at[at], glc.at[at], g2_send.at[0], g2_recv.at[at], enc=mate).wait_recv()
    total = glc[0].astype(F32)
    for c in range(1, n_col):
        total = total + glc[c].astype(F32)
    mine = me_e * n_row + me_r
    glf[mine] = total.astype(BF16)

    def gl_all(de, dr):
        return remote(glf.at[mine], glf.at[mine], g3_send.at[de * n_row + dr], g3_recv.at[mine],
                      enc=lax.rem(me_e + de, 2), row=row_of(dr))

    others = [(de, dr) for de in range(2) for dr in range(n_row) if de or dr]
    for de, dr in others:
        gl_all(de, dr).start()
    for de, dr in others:
        at = lax.rem(me_e + de, 2) * n_row + row_of(dr)
        remote(glf.at[at], glf.at[at], g3_send.at[0], g3_recv.at[at], enc=mate).wait_recv()
    for e in range(2):
        for r in range(n_row):
            gl_o[r * chunk:(r + 1) * chunk, e * width:(e + 1) * width] = (
                glf[e * n_row + r].astype(F32))
    gl_copy = pltpu.make_async_copy(gl_o, gl_h, out_sem.at[1])
    gl_copy.start()
    act_copy.wait()
    ge_copy.wait()

    for c in range(n_col):
        @pl.when(jnp.logical_and(c <= me_c, me_c < n_col - 1))
        def _():
            feat_col(c, 1).wait_send()

        @pl.when(jnp.logical_and(c >= me_c, me_c > 0))
        def _():
            feat_col(c, -1).wait_send()

    for d in range(1, n_col):
        back_col(d).wait_send()
        gl_col(d).wait_send()
    for d in range(1, n_row):
        gl_row(d).wait_send()
    for de, dr in others:
        gl_all(de, dr).wait_send()

    def drain(step, carry):
        dc = step // (n_row - 1)
        dr = step % (n_row - 1) + 1
        feat_row(dc, dr).wait_send()
        back_row(dc, dr).wait_send()
        return carry

    lax.fori_loop(0, n_col * (n_row - 1), drain, 0)
    gl_copy.wait()


def hand_out(a, b, c, a_out, b_out, c_out, a_mid, b_mid, c_mid, in_sem, out_sem):
    ways = [(a, a_mid, a_out), (b, b_mid, b_out), (c, c_mid, c_out)]
    ins = [pltpu.make_async_copy(x, y, in_sem.at[i]) for i, (x, y, _) in enumerate(ways)]
    outs = [pltpu.make_async_copy(y, z, out_sem.at[i]) for i, (_, y, z) in enumerate(ways)]
    for copy in ins:
        copy.start()
    for before, after in zip(ins, outs):
        before.wait()
        after.start()
    for copy in outs:
        copy.wait()


def on_device(embedding, w_first, b_first, w_second, w_layer, block_source, block_rows,
              block_cols, block_count, block_tiles, node_order, cotangent):
    n_row = lax.axis_size("row")
    n_col = lax.axis_size("col")
    segs = n_row * n_col
    half = embedding.shape[1]
    full = embedding.shape[2]
    rows = 2 * half
    width = full // 2
    ts = block_tiles.shape[-1]
    blocks = rows // ts
    total = block_tiles.shape[1]
    hbm = pl.BlockSpec(memory_space=pltpu.HBM)
    smem = pl.BlockSpec(memory_space=pltpu.SMEM)
    dma = pltpu.SemaphoreType.DMA
    chunk = full // n_row
    scratch = [
        pltpu.VMEM((rows, width), BF16),
        pltpu.VMEM((full, full), F32),
        pltpu.VMEM((half, full), F32),
        dma((3,)),
        pltpu.VMEM((half, full), BF16),
        pltpu.VMEM((full, full), BF16),
        pltpu.VMEM((1, full), F32),
        pltpu.VMEM((full, full), BF16),
        pltpu.VMEM((full, full), BF16),
        pltpu.VMEM((total, ts, ts), BF16),
        pltpu.VMEM(node_order.shape, jnp.int32),
        pltpu.VMEM((rows, width), BF16),
        pltpu.SMEM((segs * PAIR,), jnp.int32),
        dma((8,)),
        pltpu.VMEM((half, full), F32),
        pltpu.VMEM((2, half, width), BF16),
        pltpu.VMEM((2, half, width), BF16),
        pltpu.VMEM((2, half, full), BF16),
        pltpu.VMEM((2, half, width), BF16),
        pltpu.VMEM((2, half, width), BF16),
        pltpu.VMEM((segs, blocks, ts, width), BF16),
        pltpu.VMEM((rows, width), F32),
        pltpu.VMEM((blocks, width, ts), BF16),
        pltpu.VMEM((segs, width, rows), BF16),
        pltpu.VMEM((segs, width, rows), BF16),
        pltpu.VMEM((n_col, width, rows), BF16),
        pltpu.VMEM((n_col, width, rows), BF16),
        pltpu.VMEM((width, rows), F32),
        pltpu.VMEM((n_row, chunk, width), BF16),
        pltpu.VMEM((n_row, chunk, width), BF16),
        pltpu.VMEM((n_col, chunk, width), BF16),
        pltpu.VMEM((2 * n_row, chunk, width), BF16),
        dma((3,)), dma((3,)),
        dma((2 * n_col,)), dma((segs,)), dma((segs,)),
        dma((segs,)), dma((segs,)), dma((n_col,)), dma((n_col,)),
        dma((n_row,)), dma((n_row,)), dma((n_col,)), dma((n_col,)),
        dma((2 * n_row,)), dma((2 * n_row,)),
    ]
    shapes = (
        jax.ShapeDtypeStruct((rows, width), BF16),
        jax.ShapeDtypeStruct((full, full), F32),
        jax.ShapeDtypeStruct((half, full), F32),
    )
    results = pl.pallas_call(
        functools.partial(kernel, n_row, n_col),
        out_shape=shapes,
        in_specs=[hbm] * 5 + [smem] * 4 + [hbm] * 3,
        out_specs=(hbm, hbm, hbm),
        scratch_shapes=scratch,
        compiler_params=pltpu.CompilerParams(
            collective_id=0, has_side_effects=True, vmem_limit_bytes=64 * 1024 * 1024),
    )(embedding[0], w_first, b_first[None], w_second, w_layer, block_source,
      block_rows, block_cols, block_count, block_tiles[0], node_order, cotangent[0])
    activated, grad_layer, grad_embed = pl.pallas_call(
        hand_out,
        out_shape=shapes,
        in_specs=[hbm] * 3,
        out_specs=(hbm, hbm, hbm),
        scratch_shapes=[pltpu.VMEM(x.shape, x.dtype) for x in shapes] + [dma((3,)), dma((3,))],
        compiler_params=pltpu.CompilerParams(vmem_limit_bytes=64 * 1024 * 1024),
    )(*results)
    return (activated[None], grad_layer, grad_embed[None])


def solution(mesh):
    in_specs = (
        P(("row", "col"), "enc", None),
        P(),
        P(),
        P(),
        P(),
        P(("row", "col"), None),
        P(("row", "col"), None),
        P(("row", "col"), None),
        P(("row", "col")),
        P(("row", "col"), None, None, None),
        P(None, "col", None),
        P(("row", "col"), None, "enc"),
    )
    out_specs = (P(("row", "col"), None, "enc"), P(), P(("row", "col"), "enc", None))
    return jax.shard_map(
        on_device, mesh=mesh, in_specs=in_specs, out_specs=out_specs, check_vma=False
    )
```

```python
import functools

import jax
import jax.numpy as jnp
from jax import lax
from jax.experimental import pallas as pl
from jax.experimental.pallas import tpu as pltpu
from jax.sharding import PartitionSpec as P

MESH = pl.DeviceIdType.MESH
PAIR = 3
F32 = jnp.float32
BF16 = jnp.bfloat16


def silu_slope(values):
    sigmoid = jax.nn.sigmoid(values)
    return sigmoid * (1.0 + values * (1.0 - sigmoid))


def dot(a, b, ca=1, cb=0):
    return lax.dot_general(a, b, (((ca,), (cb,)), ((), ())), preferred_element_type=F32)


def kernel(n_row, n_col, emb_h, w1_h, b1_h, w2_h, wl_h, src_h, rws_h, cls_h, cnt, tiles_h, order_h, cot_h,
           act_h, gl_h, ge_h,
           act_o, gl_o, ge_o, out_sem,
           emb, w1, b1, w2, wl, tiles, order, cot, src, rws, cls, meta, in_sem,
           first, pall, psend, eall, pgx, pgsend, feat, acc, pgt, pb, rb, sb, cb, own,
           glp, glr, glc, glf,
           m_send, m_recv, fc_send, fr_send, f_recv, br_send, br_recv, bc_send, bc_recv,
           g1_send, g1_recv, g2_send, g2_recv, g3_send, g3_recv):
    me_e = lax.axis_index("enc")
    me_r = lax.axis_index("row")
    me_c = lax.axis_index("col")
    mate = 1 - me_e
    half = emb.shape[0]
    rows = 2 * half
    width = pall.shape[2]
    ts = tiles.shape[1]

    def row_of(d):
        return lax.rem(me_r + d, n_row)

    def col_of(d):
        return lax.rem(me_c + d, n_col)

    def remote(src, dst, ssem, rsem, **dev):
        return pltpu.make_async_remote_copy(
            src_ref=src, dst_ref=dst, send_sem=ssem, recv_sem=rsem,
            device_id=dev, device_id_type=MESH)

    pairs = [(emb_h, emb), (w1_h, w1), (b1_h, b1), (w2_h, w2), (wl_h, wl), (order_h, order),
             (tiles_h, tiles), (cot_h, cot), (src_h, src), (rws_h, rws), (cls_h, cls)]
    loads = [pltpu.make_async_copy(a, b, in_sem.at[i]) for i, (a, b) in enumerate(pairs)]
    for load in loads[8:] + loads[:8]:
        load.start()

    barrier = pltpu.get_barrier_semaphore()
    pl.semaphore_signal(barrier, inc=1, device_id={"enc": mate}, device_id_type=MESH)
    for d in range(1, n_row):
        for e in range(2):
            pl.semaphore_signal(barrier, inc=1, device_id={"enc": e, "row": row_of(d)},
                                device_id_type=MESH)
    for d in range(1, n_col):
        pl.semaphore_signal(barrier, inc=1, device_id={"col": col_of(d)}, device_id_type=MESH)

    runs = src.shape[1] // PAIR

    def tabulate(seg, carry):
        at = jnp.int32(0)
        there = jnp.int32(0)
        for j in range(runs):
            hit = src[0, j * PAIR] == seg
            at = jnp.where(hit, j * PAIR, at)
            there = jnp.where(hit, 1, there)
        for k in range(PAIR):
            slot = at + k
            live = jnp.where(slot < cnt[0], there, 0)
            meta[seg * PAIR + k] = live + rws[0, slot] * 2 + cls[0, slot] * 4 + slot * 8
        return carry

    for load in loads[8:]:
        load.wait()
    lax.fori_loop(0, n_row * n_col, tabulate, 0)

    for load in loads[:6]:
        load.wait()
    linear = dot(emb[...], w1[...]) + b1[...]
    first[...] = linear
    hidden = (linear * jax.nn.sigmoid(linear)).astype(BF16)
    encoded = dot(hidden, w2[...]).astype(BF16)
    eall[me_e] = encoded
    projected = dot(encoded, wl[...]).astype(BF16)
    psend[0] = projected[:, :width]
    psend[1] = projected[:, width:]
    pall[me_e] = psend[me_e]
    node_ids = lax.broadcasted_iota(jnp.int32, (rows, rows), 0)
    perm_t = jnp.where(node_ids == order[me_r], 1.0, 0.0).astype(BF16)

    pl.semaphore_wait(barrier, 2 * n_row - 1 + n_col - 1)
    copy_p = remote(psend.at[mate], pall.at[me_e], m_send.at[0], m_recv.at[0], enc=mate)
    copy_p.start()
    copy_e = remote(eall.at[me_e], eall.at[me_e], m_send.at[1], m_recv.at[1], enc=mate)
    copy_e.start()
    copy_p.wait()

    me_slot = me_r * n_col + me_c
    grid_own = dot(perm_t, pall[...].reshape(rows, width), 0, 0).astype(BF16)
    feat[me_slot] = grid_own.reshape(rows // ts, ts, width)

    def feat_col(c, step):
        slot = me_r * n_col + c
        return remote(feat.at[slot], feat.at[slot], fc_send.at[(step + 1) // 2 * n_col + c],
                      f_recv.at[slot], col=lax.rem(me_c + step + n_col, n_col))

    def feat_row(dc, dr):
        slot = me_r * n_col + dc
        return remote(feat.at[slot], feat.at[slot], fr_send.at[dc * n_row + dr],
                      f_recv.at[slot], row=row_of(dr))

    def feat_wait(slot):
        remote(feat.at[slot], feat.at[slot], fc_send.at[0], f_recv.at[slot], enc=mate).wait_recv()

    @pl.when(me_c < n_col - 1)
    def _():
        feat_col(me_c, 1).start()

    @pl.when(me_c > 0)
    def _():
        feat_col(me_c, -1).start()

    for d in range(1, n_row):
        feat_row(me_c, d).start()

    def slots(seg):
        out = []
        for k in range(PAIR):
            m = meta[seg * PAIR + k]
            live = (m & 1) == 1
            out.append((m >> 3, live, (m >> 1) & 1, (m >> 2) & 1))
        return out

    def split(tile, live, which, axis):
        zero = jnp.zeros_like(tile)
        return jnp.concatenate(
            [jnp.where(jnp.logical_and(live, which == b), tile, zero) for b in range(rows // ts)],
            axis=axis)

    def pick(blocks, c):
        chosen = blocks[0]
        for b in range(1, len(blocks)):
            chosen = jnp.where(c == b, blocks[b], chosen)
        return chosen

    def forward(seg):
        lhs, rhs = [], []
        for index, live, r, c in slots(seg):
            lhs.append(split(tiles[index], live, r, 0))
            rhs.append(pick([feat[seg, b] for b in range(rows // ts)], c))
        return dot(jnp.concatenate(lhs, axis=1), jnp.concatenate(rhs, axis=0))

    loads[6].wait()
    acc[...] = forward(me_slot)

    def relay(d, carry):
        left = me_c - d
        right = me_c + d

        @pl.when(left >= 0)
        def _():
            feat_wait(me_r * n_col + left)

            @pl.when(me_c < n_col - 1)
            def _():
                feat_col(left, 1).start()

            for dr in range(1, n_row):
                feat_row(left, dr).start()

        @pl.when(right < n_col)
        def _():
            feat_wait(me_r * n_col + right)

            @pl.when(me_c > 0)
            def _():
                feat_col(right, -1).start()

            for dr in range(1, n_row):
                feat_row(right, dr).start()

        @pl.when(left >= 0)
        def _():
            acc[...] += forward(me_r * n_col + left)

        @pl.when(right < n_col)
        def _():
            acc[...] += forward(me_r * n_col + right)

        return carry

    lax.fori_loop(1, n_col, relay, 0)

    def nearest(k):
        low = jnp.minimum(me_c, n_col - 1 - me_c)
        d = (k + 1) // 2
        near = jnp.where(k % 2 == 1, me_c - d, me_c + d)
        far = jnp.where(me_c > n_col - 1 - me_c, n_col - 1 - k, k)
        return jnp.where(k <= 2 * low, near, far)

    def take(step, carry):
        dr = step % (n_row - 1) + 1
        slot = row_of(dr) * n_col + nearest(step // (n_row - 1))
        feat_wait(slot)
        acc[...] += forward(slot)
        return carry

    lax.fori_loop(0, n_col * (n_row - 1), take, 0)

    loads[7].wait()
    aggregated = acc[...]
    sig = jax.nn.sigmoid(aggregated)
    act_o[...] = (aggregated * sig).astype(BF16)
    act_copy = pltpu.make_async_copy(act_o, act_h, out_sem.at[0])
    act_copy.start()
    slope = sig * (1.0 + aggregated * (1.0 - sig))
    pre = cot[...].astype(F32) * slope
    for b in range(rows // ts):
        pgt[b] = pre[b * ts:(b + 1) * ts].T.astype(BF16)

    def backward(seg):
        lhs, rhs = [], []
        for index, live, r, c in slots(seg):
            lhs.append(pgt[r])
            rhs.append(split(tiles[index], live, c, 1))
        return dot(jnp.concatenate(lhs, axis=1), jnp.concatenate(rhs, axis=0))

    def back_row(dc, dr):
        slot = row_of(dr) * n_col + col_of(dc)
        there = me_r * n_col + col_of(dc)
        return remote(pb.at[slot], rb.at[there], br_send.at[dc * n_row + dr],
                      br_recv.at[there], row=row_of(dr))

    def farthest(k):
        return lax.rem(nearest(n_col - 1 - k) - me_c + n_col, n_col)

    def give(step, carry):
        dc = farthest(step // (n_row - 1))
        dr = step % (n_row - 1) + 1
        slot = row_of(dr) * n_col + col_of(dc)
        pb[slot] = backward(slot).astype(BF16)
        back_row(dc, dr).start()
        return carry

    lax.fori_loop(0, n_col * (n_row - 1), give, 0)

    def row_total(dc):
        total = backward(me_r * n_col + col_of(dc))
        for dr in range(1, n_row):
            slot = row_of(dr) * n_col + col_of(dc)
            remote(rb.at[slot], rb.at[slot], br_send.at[0], br_recv.at[slot], enc=mate).wait_recv()
            total = total + rb[slot].astype(F32)
        return total

    def back_col(dc):
        return remote(sb.at[dc], cb.at[me_c], bc_send.at[dc], bc_recv.at[me_c], col=col_of(dc))

    def pass_on(k, carry):
        dc = farthest(k)
        sb[dc] = row_total(dc).astype(BF16)
        back_col(dc).start()
        return carry

    lax.fori_loop(0, n_col - 1, pass_on, 0)
    own[...] = row_total(0)

    def collect(dc, carry):
        at = col_of(dc)
        remote(cb.at[at], cb.at[at], bc_send.at[0], bc_recv.at[at], enc=mate).wait_recv()
        own[...] += cb[at].astype(F32)
        return carry

    lax.fori_loop(1, n_col, collect, 0)

    grid_grad = own[...].astype(BF16)
    node_grad = dot(perm_t, grid_grad, 1, 1).astype(BF16)
    pgsend[...] = node_grad.reshape(2, half, width)
    copy_g = remote(pgsend.at[mate], pgx.at[me_e], m_send.at[2], m_recv.at[2], enc=mate)
    copy_g.start()
    pgx[me_e] = pgsend[me_e]

    copy_e.wait()
    part = dot(eall[...].reshape(rows, eall.shape[2]), node_grad, 0, 0)
    chunk = glp.shape[1]
    glp[...] = part.astype(BF16).reshape(n_row, chunk, width)

    def gl_row(d):
        to = row_of(d)
        return remote(glp.at[to], glr.at[me_r], g1_send.at[d], g1_recv.at[me_r], row=to)

    for d in range(1, n_row):
        gl_row(d).start()

    copy_g.wait()
    full_grad = jnp.concatenate([pgx[0], pgx[1]], axis=1)
    encoded_grad = dot(full_grad, wl[...], 1, 1).astype(BF16)
    hidden_grad = (dot(encoded_grad, w2[...], 1, 1) * silu_slope(first[...])).astype(BF16)
    ge_o[...] = dot(hidden_grad, w1[...], 1, 1)
    ge_copy = pltpu.make_async_copy(ge_o, ge_h, out_sem.at[2])
    ge_copy.start()

    total = glp[me_r].astype(F32)
    for d in range(1, n_row):
        at = row_of(d)
        remote(glr.at[at], glr.at[at], g1_send.at[0], g1_recv.at[at], enc=mate).wait_recv()
        total = total + glr[at].astype(F32)
    glc[me_c] = total.astype(BF16)

    def gl_col(d):
        return remote(glc.at[me_c], glc.at[me_c], g2_send.at[d], g2_recv.at[me_c], col=col_of(d))

    for d in range(1, n_col):
        gl_col(d).start()
    for d in range(1, n_col):
        at = col_of(d)
        remote(glc.at[at], glc.at[at], g2_send.at[0], g2_recv.at[at], enc=mate).wait_recv()
    total = glc[0].astype(F32)
    for c in range(1, n_col):
        total = total + glc[c].astype(F32)
    mine = me_e * n_row + me_r
    glf[mine] = total.astype(BF16)

    def gl_all(de, dr):
        return remote(glf.at[mine], glf.at[mine], g3_send.at[de * n_row + dr], g3_recv.at[mine],
                      enc=lax.rem(me_e + de, 2), row=row_of(dr))

    others = [(de, dr) for de in range(2) for dr in range(n_row) if de or dr]
    for de, dr in others:
        gl_all(de, dr).start()
    for de, dr in others:
        at = lax.rem(me_e + de, 2) * n_row + row_of(dr)
        remote(glf.at[at], glf.at[at], g3_send.at[0], g3_recv.at[at], enc=mate).wait_recv()
    for e in range(2):
        for r in range(n_row):
            gl_o[r * chunk:(r + 1) * chunk, e * width:(e + 1) * width] = (
                glf[e * n_row + r].astype(F32))
    gl_copy = pltpu.make_async_copy(gl_o, gl_h, out_sem.at[1])
    gl_copy.start()
    act_copy.wait()
    ge_copy.wait()

    for c in range(n_col):
        @pl.when(jnp.logical_and(c <= me_c, me_c < n_col - 1))
        def _():
            feat_col(c, 1).wait_send()

        @pl.when(jnp.logical_and(c >= me_c, me_c > 0))
        def _():
            feat_col(c, -1).wait_send()

    for d in range(1, n_col):
        back_col(d).wait_send()
        gl_col(d).wait_send()
    for d in range(1, n_row):
        gl_row(d).wait_send()
    for de, dr in others:
        gl_all(de, dr).wait_send()

    def drain(step, carry):
        dc = step // (n_row - 1)
        dr = step % (n_row - 1) + 1
        feat_row(dc, dr).wait_send()
        back_row(dc, dr).wait_send()
        return carry

    lax.fori_loop(0, n_col * (n_row - 1), drain, 0)
    gl_copy.wait()


def hand_out(a, b, c, a_out, b_out, c_out, a_mid, b_mid, c_mid, in_sem, out_sem):
    ways = [(a, a_mid, a_out), (b, b_mid, b_out), (c, c_mid, c_out)]
    ins = [pltpu.make_async_copy(x, y, in_sem.at[i]) for i, (x, y, _) in enumerate(ways)]
    outs = [pltpu.make_async_copy(y, z, out_sem.at[i]) for i, (_, y, z) in enumerate(ways)]
    for copy in ins:
        copy.start()
    for before, after in zip(ins, outs):
        before.wait()
        after.start()
    for copy in outs:
        copy.wait()


def on_device(embedding, w_first, b_first, w_second, w_layer, block_source, block_rows,
              block_cols, block_count, block_tiles, node_order, cotangent):
    n_row = lax.axis_size("row")
    n_col = lax.axis_size("col")
    segs = n_row * n_col
    half = embedding.shape[1]
    full = embedding.shape[2]
    rows = 2 * half
    width = full // 2
    ts = block_tiles.shape[-1]
    blocks = rows // ts
    total = block_tiles.shape[1]
    hbm = pl.BlockSpec(memory_space=pltpu.HBM)
    smem = pl.BlockSpec(memory_space=pltpu.SMEM)
    dma = pltpu.SemaphoreType.DMA
    chunk = full // n_row
    scratch = [
        pltpu.VMEM((rows, width), BF16),
        pltpu.VMEM((full, full), F32),
        pltpu.VMEM((half, full), F32),
        dma((3,)),
        pltpu.VMEM((half, full), BF16),
        pltpu.VMEM((full, full), BF16),
        pltpu.VMEM((1, full), F32),
        pltpu.VMEM((full, full), BF16),
        pltpu.VMEM((full, full), BF16),
        pltpu.VMEM((total, ts, ts), BF16),
        pltpu.VMEM(node_order.shape, jnp.int32),
        pltpu.VMEM((rows, width), BF16),
        pltpu.SMEM((1, total), jnp.int32),
        pltpu.SMEM((1, total), jnp.int32),
        pltpu.SMEM((1, total), jnp.int32),
        pltpu.SMEM((segs * PAIR,), jnp.int32),
        dma((11,)),
        pltpu.VMEM((half, full), F32),
        pltpu.VMEM((2, half, width), BF16),
        pltpu.VMEM((2, half, width), BF16),
        pltpu.VMEM((2, half, full), BF16),
        pltpu.VMEM((2, half, width), BF16),
        pltpu.VMEM((2, half, width), BF16),
        pltpu.VMEM((segs, blocks, ts, width), BF16),
        pltpu.VMEM((rows, width), F32),
        pltpu.VMEM((blocks, width, ts), BF16),
        pltpu.VMEM((segs, width, rows), BF16),
        pltpu.VMEM((segs, width, rows), BF16),
        pltpu.VMEM((n_col, width, rows), BF16),
        pltpu.VMEM((n_col, width, rows), BF16),
        pltpu.VMEM((width, rows), F32),
        pltpu.VMEM((n_row, chunk, width), BF16),
        pltpu.VMEM((n_row, chunk, width), BF16),
        pltpu.VMEM((n_col, chunk, width), BF16),
        pltpu.VMEM((2 * n_row, chunk, width), BF16),
        dma((3,)), dma((3,)),
        dma((2 * n_col,)), dma((segs,)), dma((segs,)),
        dma((segs,)), dma((segs,)), dma((n_col,)), dma((n_col,)),
        dma((n_row,)), dma((n_row,)), dma((n_col,)), dma((n_col,)),
        dma((2 * n_row,)), dma((2 * n_row,)),
    ]
    shapes = (
        jax.ShapeDtypeStruct((rows, width), BF16),
        jax.ShapeDtypeStruct((full, full), F32),
        jax.ShapeDtypeStruct((half, full), F32),
    )
    results = pl.pallas_call(
        functools.partial(kernel, n_row, n_col),
        out_shape=shapes,
        in_specs=[hbm] * 8 + [smem] + [hbm] * 3,
        out_specs=(hbm, hbm, hbm),
        scratch_shapes=scratch,
        compiler_params=pltpu.CompilerParams(
            collective_id=0, has_side_effects=True, vmem_limit_bytes=64 * 1024 * 1024),
    )(embedding[0], w_first, b_first[None], w_second, w_layer, block_source,
      block_rows, block_cols, block_count, block_tiles[0], node_order, cotangent[0])
    activated, grad_layer, grad_embed = pl.pallas_call(
        hand_out,
        out_shape=shapes,
        in_specs=[hbm] * 3,
        out_specs=(hbm, hbm, hbm),
        scratch_shapes=[pltpu.VMEM(x.shape, x.dtype) for x in shapes] + [dma((3,)), dma((3,))],
        compiler_params=pltpu.CompilerParams(vmem_limit_bytes=64 * 1024 * 1024),
    )(*results)
    return (activated[None], grad_layer, grad_embed[None])


def solution(mesh):
    in_specs = (
        P(("row", "col"), "enc", None),
        P(),
        P(),
        P(),
        P(),
        P(("row", "col"), None),
        P(("row", "col"), None),
        P(("row", "col"), None),
        P(("row", "col")),
        P(("row", "col"), None, None, None),
        P(None, "col", None),
        P(("row", "col"), None, "enc"),
    )
    out_specs = (P(("row", "col"), None, "enc"), P(), P(("row", "col"), "enc", None))
    return jax.shard_map(
        on_device, mesh=mesh, in_specs=in_specs, out_specs=out_specs, check_vma=False
    )
```
